32 devices in a mesh: row: 8 (over z, x), col: 4 (over y, core).
Axes of the slice: x: 2, y: 2, z: 4, core: 2. Of those that a mesh axis runs over, the one named last changes fastest.
Arguments:
- input_picture: bfloat16 [128, 512, 256], P('row', 'col'), may hold values from -6 to 6
- spatial_taps_first: bfloat16 [2, 49, 256], replicated, may hold values from -0.875 to 0.875
- widening_matrix_first: bfloat16 [2, 256, 1024], replicated, may hold values from -0.375 to 0.375
- narrowing_matrix_first: bfloat16 [2, 1024, 256], replicated, may hold values from -0.1875 to 0.1875
- stride_kernel_matrix: bfloat16 [1024, 512], replicated, may hold values from -0.1875 to 0.1875
- spatial_taps_second: bfloat16 [2, 49, 512], replicated, may hold values from -0.875 to 0.875
- widening_matrix_second: bfloat16 [2, 512, 2048], replicated, may hold values from -0.25 to 0.25
- narrowing_matrix_second: bfloat16 [2, 2048, 512], replicated, may hold values from -0.125 to 0.125
- sky_clarity_marks: int32 [1, 4], replicated, may hold values 0 or 1
Outputs:
- features: bfloat16 [64, 256, 512], P('row', 'col')
The draws below stay inside these ranges and needn't reach their ends.
Inputs may be any that keep to these rules, and one draw needn't show every extreme that they name: `sky_clarity_marks`: 1 marks a tile of 64 x 64 section-two pixels whose blocks are applied, 0 a cloudy tile that passes through section two unchanged.
All inputs are finite; a program needn't handle non-finite values.
Results may differ from the reference program's by a relative error of at most 0.022.
Values may be sent and summed in bfloat16 or wider, within the bound.
A program may use at most 128 MiB of HBM per device.

```python
import jax
import jax.numpy as jnp
from jax import lax

FIRST_DEPTH = 256
SECOND_DEPTH = 512
HID1 = 1024
HID2 = 2048
NB1 = 2
NB2 = 2
TILE2 = 64
R_DEV = 16
H = 128
W = 512
H2 = 64
W2 = 256


def touch_ends(array, key, least, high):
    longest = array.shape.index(max(array.shape))
    spots = []
    for shift in (0, 1):
        where = [jax.random.randint(jax.random.fold_in(key, axis), (), 0, length) for axis, length in enumerate(array.shape)]
        where[longest] = (where[longest] + shift) % array.shape[longest]
        spots.append(tuple(where))
    return array.at[spots[0]].set(least).at[spots[1]].set(high)


def block_scale(own_key, dims, pieces, smallest, top_value):
    def one(dim, parts):
        heights = jax.random.uniform(jax.random.fold_in(jax.random.fold_in(own_key, 6), dim), (parts,), jnp.float32, smallest / len(pieces), top_value / len(pieces))
        return jnp.repeat(jnp.exp(heights), dims[dim] // parts).reshape((-1,) + (1,) * (len(dims) - dim - 1))

    level = one(*pieces[0])
    for cut in pieces[1:]:
        level = level * one(*cut)
    return level


def noise(own_key, shape, width, reach, cuts=(), kind=jnp.bfloat16):
    array = width * jax.random.normal(own_key, shape, jnp.float32)
    if cuts:
        array = array * block_scale(own_key, shape, cuts, -0.22, 0.18)
    return jnp.clip(array, -reach, reach).astype(kind)


def setup_inputs(seed: int = 0) -> dict:
    keys = jax.random.split(jax.random.key(seed), 10)
    return {
        "input_picture": noise(keys[0], (H, W, FIRST_DEPTH), 1.0, 6.0, ((0, 8), (1, 4))),
        "spatial_taps_first": noise(keys[1], (NB1, 49, FIRST_DEPTH), 49 ** -0.5, 0.875),
        "widening_matrix_first": noise(keys[2], (NB1, FIRST_DEPTH, HID1), FIRST_DEPTH ** -0.5, 0.375),
        "narrowing_matrix_first": noise(keys[3], (NB1, HID1, FIRST_DEPTH), HID1 ** -0.5, 0.1875),
        "stride_kernel_matrix": noise(keys[4], (4 * FIRST_DEPTH, SECOND_DEPTH), (4 * FIRST_DEPTH) ** -0.5, 0.1875),
        "spatial_taps_second": noise(keys[5], (NB2, 49, SECOND_DEPTH), 49 ** -0.5, 0.875),
        "widening_matrix_second": noise(keys[6], (NB2, SECOND_DEPTH, HID2), SECOND_DEPTH ** -0.5, 0.25),
        "narrowing_matrix_second": noise(keys[7], (NB2, HID2, SECOND_DEPTH), HID2 ** -0.5, 0.125),
        "sky_clarity_marks": touch_ends((jax.random.randint(keys[8], (H2 // TILE2, W2 // TILE2), 0, 2) < 1).astype(jnp.int32), jax.random.fold_in(keys[8], 1), 0, 1),
    }


epsilon = 1e-06

def depthwise(padded, kernel_taps, vertical_extent, lateral_extent):
    weights = kernel_taps.astype(jnp.float32)
    accumulated = jnp.zeros((vertical_extent, lateral_extent, padded.shape[-1]), jnp.float32)
    for tap_row in range(7):
        for tap_col in range(7):
            window = padded[tap_row:tap_row + vertical_extent, tap_col:tap_col + lateral_extent, :].astype(jnp.float32)
            accumulated = accumulated + window * weights[7 * tap_row + tap_col]
    return accumulated

def normalize(values):
    mean_pooled = lax.optimization_barrier(jnp.mean(values, axis=-1, keepdims=True))
    centred = values - mean_pooled
    variance = lax.optimization_barrier(jnp.mean(centred * centred, axis=-1, keepdims=True))
    return centred / jnp.sqrt(variance + epsilon)

def expand(flattened, w_in, w_out):
    hidden = jax.nn.gelu(jnp.dot(flattened, w_in, preferred_element_type=jnp.float32), approximate=False).astype(jnp.bfloat16)
    return jnp.dot(hidden, w_out, preferred_element_type=jnp.float32)

def block_branch(padded, kernel_taps, w_in, w_out, vertical_extent, lateral_extent):
    channels = padded.shape[-1]
    mixture = depthwise(padded, kernel_taps, vertical_extent, lateral_extent)
    flattened = normalize(mixture).astype(jnp.bfloat16).reshape(vertical_extent * lateral_extent, channels)
    return expand(flattened, w_in, w_out).reshape(vertical_extent, lateral_extent, channels)

def whole_branch(activation_tensor, kernel_taps, w_in, w_out, band_rows):
    vertical_extent, lateral_extent, channels = activation_tensor.shape
    padded = jnp.pad(activation_tensor, ((3, 3), (3, 3), (0, 0)))

    def one_band(band_index):
        first_row = (band_index * band_rows).astype(jnp.int32)
        portion = lax.dynamic_slice_in_dim(padded, first_row, band_rows + 6, 0)
        return block_branch(portion, kernel_taps, w_in, w_out, band_rows, lateral_extent)
    bands = lax.map(one_band, jnp.arange(vertical_extent // band_rows, dtype=jnp.int32))
    return bands.reshape(vertical_extent, lateral_extent, channels)

def halve_spacing(activation_tensor, stride_kernel_matrix):
    vertical_extent, lateral_extent, channels = activation_tensor.shape
    normed = normalize(activation_tensor.astype(jnp.float32)).astype(jnp.bfloat16)
    patch_blocks = normed.reshape(vertical_extent // 2, 2, lateral_extent // 2, 2, channels).transpose(0, 2, 1, 3, 4)
    patch_blocks = patch_blocks.reshape(vertical_extent // 2 * (lateral_extent // 2), 4 * channels)
    final_answer = jnp.dot(patch_blocks, stride_kernel_matrix, preferred_element_type=jnp.float32).astype(jnp.bfloat16)
    return final_answer.reshape(vertical_extent // 2, lateral_extent // 2, stride_kernel_matrix.shape[1])

def reference(input_picture, spatial_taps_first, widening_matrix_first, narrowing_matrix_first, stride_kernel_matrix, spatial_taps_second, widening_matrix_second, narrowing_matrix_second, sky_clarity_marks):
    running_activation = input_picture
    for layer_index in range(NB1):
        branch = whole_branch(running_activation, spatial_taps_first[layer_index], widening_matrix_first[layer_index], narrowing_matrix_first[layer_index], R_DEV)
        running_activation = (running_activation.astype(jnp.float32) + branch).astype(jnp.bfloat16)
    halved_lattice = halve_spacing(running_activation, stride_kernel_matrix)
    keep = jnp.repeat(jnp.repeat(sky_clarity_marks, TILE2, axis=0), TILE2, axis=1) == 1
    for layer_index in range(NB2):
        branch = whole_branch(halved_lattice, spatial_taps_second[layer_index], widening_matrix_second[layer_index], narrowing_matrix_second[layer_index], R_DEV // 2)
        updated = (halved_lattice.astype(jnp.float32) + branch).astype(jnp.bfloat16)
        halved_lattice = jnp.where(keep[:, :, None], updated, halved_lattice)
    return halved_lattice
```

```python
import functools

import jax
import jax.numpy as jnp
from jax import lax
from jax.experimental import pallas as pl
from jax.experimental.pallas import tpu as pltpu
from jax.sharding import PartitionSpec as P

TILE2 = 64
EPSILON = 1e-06
HALO = 3
COLS = 16
ERF_FIT = (0.7976901192585555, 0.03673081477632814, -0.0002550994688061032, -8.607627436402819e-06)
ERF_END = 25.0
SIDES = ((-1, 0), (1, 0), (0, -1), (0, 1), (-1, -1), (-1, 1), (1, -1), (1, 1))
f32 = jnp.float32
bf16 = jnp.bfloat16


def first_block(tap_col):
    return 0 if tap_col < 3 else 1


def tap_blocks(tap_col, wide):
    return wide if tap_col == 3 else wide + 1


def slot_offset(tap_col, wide):
    return sum(tap_blocks(b, wide) for b in range(tap_col))


def kernel(
    count_rows,
    count_cols,
    x_hbm, t1_hbm, a1_hbm, b1_hbm, sk_hbm, t2_hbm, a2_hbm, b2_hbm, flag_ref,
    out_ref,
    x0, x1, z0, z1, t1, a1, b1, sk, t2, a2, b2,
    kb1, kb2, sum1, sum2, shift1, shift2, split, patches,
    load_sem, send_sem, recv_sem,
):
    rows_one = x0.shape[0] - 2 * HALO
    rows_two = z0.shape[0] - 2 * HALO
    wide_one = x0.shape[1] - 2
    wide_two = z0.shape[1] - 2
    c_one = x0.shape[-1]
    c_two = z0.shape[-1]
    me_row = lax.axis_index("row")
    me_col = lax.axis_index("col")

    def exists(dr, dc):
        ok = None
        for step, me, count in ((dr, me_row, count_rows), (dc, me_col, count_cols)):
            if step == 0:
                continue
            here = me > 0 if step < 0 else me < count - 1
            ok = here if ok is None else jnp.logical_and(ok, here)
        return ok

    loads = []
    for index, (src, dst) in enumerate(
        (
            (x_hbm, x0.at[pl.ds(HALO, rows_one), pl.ds(1, wide_one)]),
            (t1_hbm, t1), (a1_hbm, a1), (b1_hbm, b1),
            (sk_hbm, sk), (t2_hbm, t2), (a2_hbm, a2), (b2_hbm, b2),
        )
    ):
        copy = pltpu.make_async_copy(src, dst, load_sem.at[index])
        copy.start()
        loads.append(copy)

    barrier = pltpu.get_barrier_semaphore()
    total = jnp.int32(0)
    for dr, dc in SIDES:
        near = exists(dr, dc)

        @pl.when(near)
        def _(dr=dr, dc=dc):
            pl.semaphore_signal(
                barrier, inc=1, device_id=(me_row + dr, me_col + dc), device_id_type=pl.DeviceIdType.MESH
            )

        total = total + jnp.where(near, 1, 0)
    pl.semaphore_wait(barrier, total)

    def transfer(which, side, source=None):
        dr, dc = SIDES[side]
        field = (x0, x1, z0, z1)[which]
        rows = field.shape[0] - 2 * HALO
        wide = field.shape[1] - 2
        from_row = {-1: 0, 0: 0, 1: rows - HALO}[dr]
        to_row = {-1: HALO + rows, 0: HALO, 1: 0}[dr]
        n_rows = HALO if dr else rows
        from_block = {-1: 0, 0: 0, 1: wide - 1}[dc]
        to_block = {-1: wide + 1, 0: 1, 1: 0}[dc]
        n_blocks = 1 if dc else wide
        if source is None:
            src = field.at[pl.ds(HALO + from_row, n_rows), pl.ds(1 + from_block, n_blocks)]
        else:
            src = source.at[pl.ds(from_row, n_rows), pl.ds(from_block, n_blocks)]
        return pltpu.make_async_remote_copy(
            src_ref=src,
            dst_ref=field.at[pl.ds(to_row, n_rows), pl.ds(to_block, n_blocks)],
            send_sem=send_sem.at[which, side],
            recv_sem=recv_sem.at[which, side],
            device_id=(
                jnp.clip(me_row + dr, 0, count_rows - 1),
                jnp.clip(me_col + dc, 0, count_cols - 1),
            ),
            device_id_type=pl.DeviceIdType.MESH,
        )

    def send(which, sides, source=None):
        for side in sides:
            @pl.when(exists(*SIDES[side]))
            def _(side=side):
                transfer(which, side, source).start()

    def arrive(which, sides):
        for side in sides:
            dr, dc = SIDES[side]

            @pl.when(exists(-dr, -dc))
            def _(side=side):
                transfer(which, side).wait_recv()

    def sent(which, source=None):
        for side in range(len(SIDES)):
            @pl.when(exists(*SIDES[side]))
            def _(side=side):
                transfer(which, side, source).wait_send()

    COLUMN_SIDES = (2, 3)
    OTHER_SIDES = (0, 1, 4, 5, 6, 7)
    send(0, COLUMN_SIDES + OTHER_SIDES, x_hbm)

    for field in (x0, x1, z0, z1):
        rows = field.shape[0] - 2 * HALO
        wide = field.shape[1] - 2
        row_band = jnp.zeros((HALO,) + field.shape[1:], bf16)
        col_band = jnp.zeros((field.shape[0],) + field.shape[2:], bf16)

        @pl.when(me_row == 0)
        def _(field=field, row_band=row_band):
            field[0:HALO] = row_band

        @pl.when(me_row == count_rows - 1)
        def _(field=field, row_band=row_band, rows=rows):
            field[HALO + rows : 2 * HALO + rows] = row_band

        @pl.when(me_col == 0)
        def _(field=field, col_band=col_band):
            field[:, 0] = col_band

        @pl.when(me_col == count_cols - 1)
        def _(field=field, col_band=col_band, wide=wide):
            field[:, wide + 1] = col_band

    def build_shift(ref, wide):
        shape = ref.shape
        gap = lax.broadcasted_iota(jnp.int32, shape, 1) - lax.broadcasted_iota(jnp.int32, shape, 0)
        hit = jnp.zeros(shape, f32)
        for b in range(7):
            start = (slot_offset(b, wide) - first_block(b)) * COLS + COLS - HALO + b
            hit = jnp.where(gap == start, 1.0, hit)
        ref[...] = hit.astype(bf16)

    build_shift(shift1, wide_one)
    build_shift(shift2, wide_two)
    width = split.shape[0]
    target = lax.broadcasted_iota(jnp.int32, split.shape, 0)
    picked = jnp.where(target < width // 2, 2 * target, 2 * target - width + 1)
    split[...] = jnp.where(lax.broadcasted_iota(jnp.int32, split.shape, 1) == picked, 1.0, 0.0).astype(bf16)

    def spread_taps(dst, src):
        for layer in range(src.shape[0]):
            wide_taps = src[layer].astype(f32)
            for tap in range(49):
                dst[layer, tap] = jnp.broadcast_to(wide_taps[tap : tap + 1], dst.shape[2:]).astype(bf16)

    def centre(values):
        c = values.shape[-1]
        ones = jnp.full((c, c), 1.0 / c, bf16)
        mean = jnp.dot(values.astype(bf16), ones, preferred_element_type=f32)
        centred = values - mean
        variance = jnp.dot((centred * centred).astype(bf16), ones, preferred_element_type=f32)
        return (centred * lax.rsqrt(variance + EPSILON)).astype(bf16)

    def gelu_twice(h):
        square = jnp.minimum(h * h, ERF_END)
        q = ERF_FIT[3]
        for term in ERF_FIT[2::-1]:
            q = q * square + term
        return h + h * jnp.tanh(h * q)

    def branch_rows(field, taps, w_in, w_out, sums, shift, layer, row, n):
        wide = field.shape[1] - 2
        c = field.shape[-1]

        def one_block(block, taps_in_row):
            for lane in range(c // 128):
                lanes = slice(lane * 128, (lane + 1) * 128)
                cells = [field[row + r, block, :, lanes] for r in range(n + 2 * HALO)]
                for b in taps_in_row:
                    tap = [taps[layer, 7 * a + b, :, lanes] for a in range(7)]
                    for r in range(n):
                        p = [cells[r + a] * tap[a] for a in range(7)]
                        total = ((p[0] + p[1]) + (p[2] + p[3])) + ((p[4] + p[5]) + p[6])
                        sums[r, slot_offset(b, wide) - first_block(b) + block, :, lanes] = total

        one_block(0, range(0, 3))
        one_block(wide + 1, range(4, 7))

        @pl.loop(1, wide + 1)
        def _(block):
            one_block(block, range(7))

        slots = slot_offset(7, wide)
        mixed = [
            jnp.dot(shift[...], sums[r].reshape(slots * COLS, c), preferred_element_type=f32)
            for r in range(n)
        ]
        flat = centre(jnp.concatenate(mixed, axis=0))
        hidden_size = w_in.shape[-1]
        step = 512
        total = None
        for k in range(0, hidden_size, step):
            h = jnp.dot(flat, w_in[layer, :, k : k + step], preferred_element_type=f32)
            g = gelu_twice(h).astype(bf16)
            part = jnp.dot(g, w_out[layer, k : k + step, :], preferred_element_type=f32)
            total = part if total is None else total + part
        return 0.5 * total

    def plain(field, row, n):
        wide = field.shape[1] - 2
        c = field.shape[-1]
        return field[pl.ds(HALO + row, n), 1 : 1 + wide].astype(f32).reshape(n * wide * COLS, c)

    def section_one(layer, row, n):
        field = (x0, x1)[layer]
        branch = branch_rows(field, kb1, a1, b1, sum1, shift1, layer, row, n)
        new = (plain(field, row, n) + branch).astype(bf16)
        if layer == 0:
            x1[pl.ds(HALO + row, n), 1 : 1 + wide_one] = new.reshape(n, wide_one, COLS, c_one)
        else:
            normed = centre(new.astype(f32))
            for r in range(n):
                both = jnp.dot(
                    split[...], normed[r * width : (r + 1) * width], preferred_element_type=f32
                ).astype(bf16)
                place = row + r
                first = 2 * lax.rem(place, 2)
                patches[first, lax.div(place, 2)] = both[: width // 2]
                patches[first + 1, lax.div(place, 2)] = both[width // 2 :]

    def section_two(layer, row, n):
        field = (z0, z1)[layer]
        branch = branch_rows(field, kb2, a2, b2, sum2, shift2, layer, row, n)
        old = plain(field, row, n)
        keep = jnp.broadcast_to(flag_ref[0:1, :], old.shape) > 0.5
        new = jnp.where(keep, old + branch, old).astype(bf16).reshape(n, wide_two, COLS, c_two)
        if layer == 0:
            z1[pl.ds(HALO + row, n), 1 : 1 + wide_two] = new
        else:
            out_ref[pl.ds(row, n)] = new

    def run(work, which, layer, rows, per_step):
        arrive(which, COLUMN_SIDES)

        @pl.loop(0, (rows - 2 * HALO) // per_step)
        def _(index):
            work(layer, HALO + index * per_step, per_step)

        arrive(which, OTHER_SIDES)

        @pl.loop(0, 2)
        def _(index):
            work(layer, index * (rows - HALO), HALO)

    loads[1].wait()
    spread_taps(kb1, t1)
    loads[0].wait()
    loads[2].wait()
    loads[3].wait()
    run(section_one, 0, 0, rows_one, 2)
    send(1, COLUMN_SIDES + OTHER_SIDES)
    loads[5].wait()
    spread_taps(kb2, t2)
    run(section_one, 1, 1, rows_one, 2)

    loads[4].wait()
    together = 4 if rows_two % 4 == 0 else 1

    @pl.loop(0, rows_two // together)
    def _(index):
        total = None
        for q in range(4):
            patch = patches[q, pl.ds(index * together, together)].reshape(together * (width // 2), c_one)
            part = jnp.dot(patch, sk[q * c_one : (q + 1) * c_one], preferred_element_type=f32)
            total = part if total is None else total + part
        z0[pl.ds(HALO + index * together, together), 1 : 1 + wide_two] = total.astype(bf16).reshape(
            together, wide_two, COLS, c_two
        )

    send(2, COLUMN_SIDES + OTHER_SIDES)
    loads[6].wait()
    loads[7].wait()
    run(section_two, 2, 0, rows_two, 2)
    send(3, COLUMN_SIDES + OTHER_SIDES)
    run(section_two, 3, 1, rows_two, 2)
    sent(0, x_hbm)
    for which in range(1, 4):
        sent(which)


def per_device(
    count_rows,
    count_cols,
    input_picture,
    spatial_taps_first,
    widening_matrix_first,
    narrowing_matrix_first,
    stride_kernel_matrix,
    spatial_taps_second,
    widening_matrix_second,
    narrowing_matrix_second,
    sky_clarity_marks,
):
    rows, cols, c_one = input_picture.shape
    c_two = stride_kernel_matrix.shape[1]
    wide_one = cols // COLS
    wide_two = cols // (2 * COLS)
    tile_row = lax.axis_index("row") * (rows // 2) // TILE2
    tile_col = lax.axis_index("col") * (cols // 2) // TILE2
    flag = lax.dynamic_slice(sky_clarity_marks, (tile_row, tile_col), (1, 1))
    flag = jnp.broadcast_to((flag == 1).astype(f32), (8, c_two))
    slots_one = slot_offset(7, wide_one)
    slots_two = slot_offset(7, wide_two)
    weights = (
        spatial_taps_first, widening_matrix_first, narrowing_matrix_first, stride_kernel_matrix,
        spatial_taps_second, widening_matrix_second, narrowing_matrix_second,
    )
    vmem = pltpu.VMEM
    out = pl.pallas_call(
        functools.partial(kernel, count_rows, count_cols),
        out_shape=jax.ShapeDtypeStruct((rows // 2, wide_two, COLS, c_two), bf16),
        in_specs=[pl.BlockSpec(memory_space=pl.ANY)] * 8 + [pl.BlockSpec(memory_space=vmem)],
        out_specs=pl.BlockSpec(memory_space=vmem),
        scratch_shapes=[
            vmem((rows + 2 * HALO, wide_one + 2, COLS, c_one), bf16),
            vmem((rows + 2 * HALO, wide_one + 2, COLS, c_one), bf16),
            vmem((rows // 2 + 2 * HALO, wide_two + 2, COLS, c_two), bf16),
            vmem((rows // 2 + 2 * HALO, wide_two + 2, COLS, c_two), bf16),
            *[vmem(w.shape, bf16) for w in weights],
            vmem(spatial_taps_first.shape[:2] + (COLS, c_one), bf16),
            vmem(spatial_taps_second.shape[:2] + (COLS, c_two), bf16),
            vmem((HALO, slots_one, COLS, c_one), bf16),
            vmem((HALO, slots_two, COLS, c_two), bf16),
            vmem((cols, slots_one * COLS), bf16),
            vmem((cols // 2, slots_two * COLS), bf16),
            vmem((cols, cols), bf16),
            vmem((4, rows // 2, cols // 2, c_one), bf16),
            pltpu.SemaphoreType.DMA((8,)),
            pltpu.SemaphoreType.DMA((4, len(SIDES))),
            pltpu.SemaphoreType.DMA((4, len(SIDES))),
        ],
        compiler_params=pltpu.CompilerParams(
            collective_id=0, has_side_effects=True, vmem_limit_bytes=60 * 2**20
        ),
        name="sections",
    )(input_picture.reshape(rows, wide_one, COLS, c_one), *weights, flag)
    return out.reshape(rows // 2, cols // 2, c_two)


def solution(mesh):
    placed = (P("row", "col", None), P(), P(), P(), P(), P(), P(), P(), P())
    return jax.shard_map(
        functools.partial(per_device, mesh.shape["row"], mesh.shape["col"]),
        mesh=mesh, in_specs=placed, out_specs=P("row", "col", None), check_vma=False,
    )
```

```python
import functools

import jax
import jax.numpy as jnp
from jax import lax
from jax.experimental import pallas as pl
from jax.experimental.pallas import tpu as pltpu
from jax.sharding import PartitionSpec as P

TILE2 = 64
EPSILON = 1e-06
HALO = 3
COLS = 16
ERF_FIT = (0.7975078823814434, 0.037005647651999776, -0.00035151703937969365)
ERF_END = 25.0
SIDES = ((-1, 0), (1, 0), (0, -1), (0, 1), (-1, -1), (-1, 1), (1, -1), (1, 1))
f32 = jnp.float32
bf16 = jnp.bfloat16


def largest_divisor(number, limit):
    return next(d for d in range(limit, 0, -1) if number % d == 0)


def kernel(
    count_rows,
    count_cols,
    x_hbm, t1_hbm, a1_hbm, b1_hbm, sk_hbm, t2_hbm, a2_hbm, b2_hbm, marks,
    out_ref,
    natural, e0, e1, e2, e3, h1, h2, h3, p1, p2, p3,
    t1, a1, b1, sk, t2, a2, b2,
    kb1, kb2, sum1, sum2,
    order0, fill1, fill2, pack1, pack2, unorder, patches,
    load_sem, send_sem, recv_sem,
):
    fields = (e0, e1, e2, e3)
    edges = (None, h1, h2, h3)
    packs = (None, p1, p2, p3)
    rows_one = e0.shape[0] - 2 * HALO
    rows_two = e2.shape[0] - 2 * HALO
    wide_one = e0.shape[1] - 2 * HALO
    wide_two = e2.shape[1] - 2 * HALO
    c_one = e0.shape[-1]
    c_two = e2.shape[-1]
    me_row = lax.axis_index("row")
    me_col = lax.axis_index("col")

    def exists(dr, dc):
        ok = None
        for step, me, count in ((dr, me_row, count_rows), (dc, me_col, count_cols)):
            if step == 0:
                continue
            here = me > 0 if step < 0 else me < count - 1
            ok = here if ok is None else jnp.logical_and(ok, here)
        return ok

    loads = []
    for index, (src, dst) in enumerate(
        (
            (x_hbm, natural.at[pl.ds(HALO, rows_one), pl.ds(1, wide_one)]),
            (t1_hbm, t1), (a1_hbm, a1), (b1_hbm, b1),
            (sk_hbm, sk), (t2_hbm, t2), (a2_hbm, a2), (b2_hbm, b2),
        )
    ):
        copy = pltpu.make_async_copy(src, dst, load_sem.at[index])
        copy.start()
        loads.append(copy)

    barrier = pltpu.get_barrier_semaphore()
    total = jnp.int32(0)
    for dr, dc in SIDES:
        near = exists(dr, dc)

        @pl.when(near)
        def _(dr=dr, dc=dc):
            pl.semaphore_signal(
                barrier, inc=1, device_id=(me_row + dr, me_col + dc), device_id_type=pl.DeviceIdType.MESH
            )

        total = total + jnp.where(near, 1, 0)
    pl.semaphore_wait(barrier, total)

    def transfer(which, side):
        dr, dc = SIDES[side]
        rows = fields[which].shape[0] - 2 * HALO
        wide = fields[which].shape[1] - 2 * HALO
        from_row = {-1: 0, 0: 0, 1: rows - HALO}[dr]
        to_row = {-1: HALO + rows, 0: HALO, 1: 0}[dr]
        n_rows = HALO if dr else rows
        if which == 0:
            from_block = {-1: 0, 0: 0, 1: wide - 1}[dc]
            to_block = {-1: wide + 1, 0: 1, 1: 0}[dc]
            n_blocks = 1 if dc else wide
            src = x_hbm.at[pl.ds(from_row, n_rows), pl.ds(from_block, n_blocks)]
            dst = natural.at[pl.ds(to_row, n_rows), pl.ds(to_block, n_blocks)]
        elif dc == 0:
            src = fields[which].at[pl.ds(HALO + from_row, n_rows), pl.ds(HALO, wide)]
            dst = fields[which].at[pl.ds(to_row, n_rows), pl.ds(HALO, wide)]
        else:
            src = packs[which].at[pl.ds(from_row, n_rows), pl.ds((1 + dc) // 2, 1)]
            dst = edges[which].at[pl.ds(to_row, n_rows), pl.ds((1 - dc) // 2, 1)]
        return pltpu.make_async_remote_copy(
            src_ref=src,
            dst_ref=dst,
            send_sem=send_sem.at[which, side],
            recv_sem=recv_sem.at[which, side],
            device_id=(
                jnp.clip(me_row + dr, 0, count_rows - 1),
                jnp.clip(me_col + dc, 0, count_cols - 1),
            ),
            device_id_type=pl.DeviceIdType.MESH,
        )

    def send(which):
        for side in (2, 3, 0, 1, 4, 5, 6, 7):
            @pl.when(exists(*SIDES[side]))
            def _(side=side):
                transfer(which, side).start()

    def arrive(which, sides):
        for side in sides:
            dr, dc = SIDES[side]

            @pl.when(exists(-dr, -dc))
            def _(side=side):
                transfer(which, side).wait_recv()

    def sent(which):
        for side in range(len(SIDES)):
            @pl.when(exists(*SIDES[side]))
            def _(side=side):
                transfer(which, side).wait_send()

    send(0)

    for field, left, right, inner in (
        (natural, 0, wide_one + 1, None),
        (h1, 0, 1, e1), (h2, 0, 1, e2), (h3, 0, 1, e3),
    ):
        rows = field.shape[0] - 2 * HALO
        row_band = jnp.zeros((HALO,) + field.shape[1:], bf16)
        col_band = jnp.zeros((field.shape[0],) + field.shape[2:], bf16)

        def clear_rows(first, field=field, inner=inner, row_band=row_band):
            field[first : first + HALO] = row_band
            if inner is not None:
                inner[first : first + HALO] = jnp.zeros((HALO,) + inner.shape[1:], bf16)

        @pl.when(me_row == 0)
        def _(clear_rows=clear_rows):
            clear_rows(0)

        @pl.when(me_row == count_rows - 1)
        def _(clear_rows=clear_rows, rows=rows):
            clear_rows(HALO + rows)

        @pl.when(me_col == 0)
        def _(field=field, col_band=col_band, left=left):
            field[:, left] = col_band

        @pl.when(me_col == count_cols - 1)
        def _(field=field, col_band=col_band, right=right):
            field[:, right] = col_band

    def pick(ref, source):
        wanted = source(lax.broadcasted_iota(jnp.int32, ref.shape, 0))
        column = lax.broadcasted_iota(jnp.int32, ref.shape, 1)
        ref[...] = jnp.where(column == wanted, 1.0, 0.0).astype(bf16)

    def slab_order(m):
        return (m & (COLS - 1)) * wide_one + (m >> 4) - HALO + COLS

    def fill_order(wide):
        def source(m):
            k, s = m >> 4, m & (COLS - 1)
            left = jnp.where(s == 0, wide * COLS + k, (wide - HALO + k) * COLS + s - 1)
            other = k - HALO
            right = jnp.where(s == COLS - 1, (wide + 1) * COLS + other, other * COLS + s + 1)
            return jnp.where(k < HALO, left, right)

        return source

    def pack_order(wide):
        def source(m):
            k = m & (COLS - 1)
            place = jnp.where(m < COLS, k * COLS, (wide - HALO + k) * COLS + COLS - 1)
            return jnp.where(k < HALO, place, -1)

        return source

    def natural_order(m):
        bits = wide_two.bit_length() - 1
        return (m & (wide_two - 1)) * COLS + (m >> bits)

    pick(order0, slab_order)
    pick(fill1, fill_order(wide_one))
    pick(fill2, fill_order(wide_two))
    pick(pack1, pack_order(wide_one))
    pick(pack2, pack_order(wide_two))
    pick(unorder, natural_order)

    def move(matrix, values):
        return jnp.dot(matrix[...], values, preferred_element_type=f32).astype(bf16)

    def spread_taps(dst, src):
        for tap in range(49):
            both = src[tap].astype(f32)
            for layer in range(both.shape[0]):
                dst[layer, tap] = jnp.broadcast_to(both[layer : layer + 1], dst.shape[2:]).astype(bf16)

    def fill(which, row):
        field = fields[which]
        wide = field.shape[1] - 2 * HALO
        c = field.shape[-1]
        if which == 0:
            values = natural[row].reshape((wide + 2) * COLS, c)
            field[row] = move(order0, values).reshape(wide + 2 * HALO, COLS, c)
            return
        inner = field[row, HALO : HALO + wide].reshape(wide * COLS, c)
        values = jnp.concatenate([inner, edges[which][row].reshape(2 * COLS, c)], axis=0)
        outer = move(fill1 if which == 1 else fill2, values).reshape(2 * HALO, COLS, c)
        field[row, 0:HALO] = outer[:HALO]
        field[row, HALO + wide : 2 * HALO + wide] = outer[HALO:]

    def store_field(which, row, n, new):
        field = fields[which]
        wide = field.shape[1] - 2 * HALO
        c = field.shape[-1]
        size = wide * COLS
        field[pl.ds(HALO + row, n), HALO : HALO + wide] = new.reshape(n, wide, COLS, c)
        for r in range(n):
            packed = move(pack1 if which == 1 else pack2, new[r * size : (r + 1) * size])
            packs[which][row + r] = packed.reshape(2, COLS, c)

    def centre(values):
        c = values.shape[-1]
        ones = jnp.full((c, c), 1.0 / c, bf16)
        mean = jnp.dot(values.astype(bf16), ones, preferred_element_type=f32)
        centred = values.astype(f32) - mean
        variance = jnp.dot((centred * centred).astype(bf16), ones, preferred_element_type=f32)
        return (centred * lax.rsqrt(variance + EPSILON)).astype(bf16)

    def gelu_twice(h):
        square = jnp.minimum(h * h, ERF_END)
        q = (ERF_FIT[2] * square + ERF_FIT[1]) * square + ERF_FIT[0]
        return h + h * jnp.tanh(h * q)

    def depthwise(field, taps, sums, layer, row, n):
        wide = field.shape[1] - 2 * HALO
        c = field.shape[-1]

        @pl.loop(0, wide)
        def _(slab):
            for lane in range(c // 128):
                lanes = slice(lane * 128, (lane + 1) * 128)
                stacks = [[] for _ in range(n)]
                for b in range(7):
                    cells = [field[row + r, slab + b, :, lanes] for r in range(n + 2 * HALO)]
                    tap = [taps[layer, 7 * a + b, :, lanes] for a in range(7)]
                    for r in range(n):
                        p = [cells[r + a] * tap[a] for a in range(7)]
                        stacks[r].append(((p[0] + p[1]) + (p[2] + p[3])) + ((p[4] + p[5]) + p[6]))
                        if b in (1, 3, 5):
                            top = stacks[r].pop()
                            stacks[r].append(stacks[r].pop() + top)
                        if b in (3, 6):
                            top = stacks[r].pop()
                            stacks[r].append(stacks[r].pop() + top)
                for r in range(n):
                    sums[r, slab, :, lanes] = stacks[r][0] + stacks[r][1]

        return sums[0:n].reshape(n * wide * COLS, c)

    def branch_rows(field, taps, w_in, w_out, sums, layer, row, n):
        flat = centre(depthwise(field, taps, sums, layer, row, n))
        hidden_size = w_in.shape[-1]
        step = 512
        total = None
        for k in range(0, hidden_size, step):
            h = jnp.dot(flat, w_in[layer, :, k : k + step], preferred_element_type=f32)
            g = gelu_twice(h.astype(bf16))
            part = jnp.dot(g, w_out[layer, k : k + step, :], preferred_element_type=f32)
            total = part if total is None else total + part
        return 0.5 * total

    def plain(field, row, n):
        wide = field.shape[1] - 2 * HALO
        c = field.shape[-1]
        return field[pl.ds(HALO + row, n), HALO : HALO + wide].astype(f32).reshape(n * wide * COLS, c)

    def section_one(layer, row, n):
        field = fields[layer]
        branch = branch_rows(field, kb1, a1, b1, sum1, layer, row, n)
        new = (plain(field, row, n) + branch).astype(bf16)
        if layer == 0:
            store_field(1, row, n, new)
            return
        normed = centre(new.astype(f32)).reshape(n, wide_one, COLS, c_one)
        for r in range(n):
            place = row + r
            first = 2 * lax.rem(place, 2)
            for q in range(wide_one):
                patches[first + q % 2, lax.div(place, 2), q // 2] = normed[r, q]

    def section_two(layer, row, n):
        field = fields[2 + layer]
        branch = branch_rows(field, kb2, a2, b2, sum2, layer, row, n)
        old = plain(field, row, n)
        mark = marks[lax.div(me_row * rows_two, TILE2), lax.div(me_col * (wide_two * COLS), TILE2)]
        keep = jnp.full(old.shape, mark, jnp.int32) == 1
        new = jnp.where(keep, old + branch, old).astype(bf16)
        if layer == 0:
            store_field(3, row, n, new)
            return
        size = wide_two * COLS
        for r in range(n):
            out_ref[row + r] = move(unorder, new[r * size : (r + 1) * size]).reshape(wide_two, COLS, c_two)

    def run(work, which, layer, rows):
        inner = rows - 2 * HALO
        per_step = largest_divisor(inner, 5)
        unroll = largest_divisor(rows, 4)
        arrive(which, (2, 3))

        @pl.loop(0, rows // unroll)
        def _(index):
            for r in range(unroll):
                fill(which, HALO + index * unroll + r)

        @pl.loop(0, inner // per_step)
        def _(index):
            work(layer, HALO + index * per_step, per_step)

        arrive(which, (0, 1, 4, 5, 6, 7))

        @pl.loop(0, 2)
        def _(index):
            for r in range(HALO):
                fill(which, index * (HALO + rows) + r)
            work(layer, index * (rows - HALO), HALO)

    loads[1].wait()
    spread_taps(kb1, t1)
    loads[0].wait()
    loads[2].wait()
    loads[3].wait()
    run(section_one, 0, 0, rows_one)
    send(1)
    loads[5].wait()
    spread_taps(kb2, t2)
    run(section_one, 1, 1, rows_one)

    loads[4].wait()
    together = largest_divisor(rows_two, 4)

    @pl.loop(0, rows_two // together)
    def _(index):
        total = None
        for q in range(4):
            patch = patches[q, pl.ds(index * together, together)].reshape(together * wide_two * COLS, c_one)
            part = jnp.dot(patch, sk[q * c_one : (q + 1) * c_one], preferred_element_type=f32)
            total = part if total is None else total + part
        store_field(2, index * together, together, total.astype(bf16))

    send(2)
    loads[6].wait()
    loads[7].wait()
    run(section_two, 2, 0, rows_two)
    send(3)
    run(section_two, 3, 1, rows_two)
    for which in range(4):
        sent(which)


def per_device(
    count_rows,
    count_cols,
    input_picture,
    spatial_taps_first,
    widening_matrix_first,
    narrowing_matrix_first,
    stride_kernel_matrix,
    spatial_taps_second,
    widening_matrix_second,
    narrowing_matrix_second,
    sky_clarity_marks,
):
    rows, cols, c_one = input_picture.shape
    c_two = stride_kernel_matrix.shape[1]
    half = rows // 2
    wide_one = cols // COLS
    wide_two = cols // (2 * COLS)
    weights = (
        spatial_taps_first.transpose(1, 0, 2), widening_matrix_first, narrowing_matrix_first,
        stride_kernel_matrix,
        spatial_taps_second.transpose(1, 0, 2), widening_matrix_second, narrowing_matrix_second,
    )
    vmem = pltpu.VMEM
    field_one = (rows + 2 * HALO, wide_one + 2 * HALO, COLS, c_one)
    field_two = (half + 2 * HALO, wide_two + 2 * HALO, COLS, c_two)
    layers = spatial_taps_first.shape[0]
    shapes = [
        (rows + 2 * HALO, wide_one + 2, COLS, c_one),
        field_one, field_one, field_two, field_two,
        (rows + 2 * HALO, 2, COLS, c_one),
        (half + 2 * HALO, 2, COLS, c_two),
        (half + 2 * HALO, 2, COLS, c_two),
        (rows, 2, COLS, c_one),
        (half, 2, COLS, c_two),
        (half, 2, COLS, c_two),
        *[w.shape for w in weights],
        (layers, 49, COLS, c_one),
        (layers, 49, COLS, c_two),
        (5, wide_one, COLS, c_one),
        (5, wide_two, COLS, c_two),
        ((wide_one + 2 * HALO) * COLS, (wide_one + 2) * COLS),
        (2 * HALO * COLS, (wide_one + 2) * COLS),
        (2 * HALO * COLS, (wide_two + 2) * COLS),
        (2 * COLS, wide_one * COLS),
        (2 * COLS, wide_two * COLS),
        (wide_two * COLS, wide_two * COLS),
        (4, half, wide_two, COLS, c_one),
    ]
    out = pl.pallas_call(
        functools.partial(kernel, count_rows, count_cols),
        out_shape=jax.ShapeDtypeStruct((half, wide_two, COLS, c_two), bf16),
        in_specs=[pl.BlockSpec(memory_space=pl.ANY)] * 8 + [pl.BlockSpec(memory_space=pltpu.SMEM)],
        out_specs=pl.BlockSpec(memory_space=vmem),
        scratch_shapes=[
            *[vmem(shape, bf16) for shape in shapes],
            pltpu.SemaphoreType.DMA((8,)),
            pltpu.SemaphoreType.DMA((4, len(SIDES))),
            pltpu.SemaphoreType.DMA((4, len(SIDES))),
        ],
        compiler_params=pltpu.CompilerParams(
            collective_id=0, has_side_effects=True, vmem_limit_bytes=60 * 2**20
        ),
        name="sections",
    )(input_picture.reshape(rows, wide_one, COLS, c_one), *weights, sky_clarity_marks)
    return out.reshape(half, cols // 2, c_two)


def solution(mesh):
    placed = (P("row", "col", None), P(), P(), P(), P(), P(), P(), P(), P())
    return jax.shard_map(
        functools.partial(per_device, mesh.shape["row"], mesh.shape["col"]),
        mesh=mesh, in_specs=placed, out_specs=P("row", "col", None), check_vma=False,
    )
```

```python
import functools

import jax
import jax.numpy as jnp
from jax import lax
from jax.experimental import pallas as pl
from jax.experimental.pallas import tpu as pltpu
from jax.sharding import PartitionSpec as P

TILE2 = 64
EPSILON = 1e-06
HALO = 3
COLS = 16
ERF_FIT = (0.7975078823814434, 0.037005647651999776, -0.00035151703937969365)
ERF_END = 25.0
SIDES = ((-1, 0), (1, 0), (0, -1), (0, 1), (-1, -1), (-1, 1), (1, -1), (1, 1))
TOP, INNER, BOTTOM = range(3)
MESSAGES = (
    (-1, 0, None), (-1, -1, None), (-1, 1, None),
    (1, 0, None), (1, -1, None), (1, 1, None),
    (0, -1, TOP), (0, 1, TOP), (0, -1, INNER), (0, 1, INNER), (0, -1, BOTTOM), (0, 1, BOTTOM),
)
UPWARD, DOWNWARD = (0, 1, 2), (3, 4, 5)
EDGES = ((6, 7), (8, 9), (10, 11))
f32 = jnp.float32
bf16 = jnp.bfloat16


def largest_divisor(number, limit):
    return next(d for d in range(limit, 0, -1) if number % d == 0)


def kernel(
    count_rows,
    count_cols,
    x_hbm, t1_hbm, a1_hbm, b1_hbm, sk_hbm, t2_hbm, a2_hbm, b2_hbm, marks,
    out_ref,
    natural, e0, e1, e2, e3, h1, h2, h3, p1, p2, p3,
    t1, a1, b1, sk, t2, a2, b2,
    kb1, kb2, sum1, sum2,
    order0, fill1, fill2, pack1, pack2, unorder, patches,
    load_sem, send_sem, recv_sem,
):
    fields = (e0, e1, e2, e3)
    edges = (None, h1, h2, h3)
    packs = (None, p1, p2, p3)
    rows_one = e0.shape[0] - 2 * HALO
    rows_two = e2.shape[0] - 2 * HALO
    wide_one = e0.shape[1] - 2 * HALO
    wide_two = e2.shape[1] - 2 * HALO
    c_one = e0.shape[-1]
    c_two = e2.shape[-1]
    me_row = lax.axis_index("row")
    me_col = lax.axis_index("col")

    def exists(dr, dc):
        ok = None
        for step, me, count in ((dr, me_row, count_rows), (dc, me_col, count_cols)):
            if step == 0:
                continue
            here = me > 0 if step < 0 else me < count - 1
            ok = here if ok is None else jnp.logical_and(ok, here)
        return ok

    loads = []
    for index, (src, dst) in enumerate(
        (
            (x_hbm, natural.at[pl.ds(HALO, rows_one), pl.ds(1, wide_one)]),
            (t1_hbm, t1), (a1_hbm, a1), (b1_hbm, b1),
            (sk_hbm, sk), (t2_hbm, t2), (a2_hbm, a2), (b2_hbm, b2),
        )
    ):
        copy = pltpu.make_async_copy(src, dst, load_sem.at[index])
        copy.start()
        loads.append(copy)

    barrier = pltpu.get_barrier_semaphore()
    total = jnp.int32(0)
    for dr, dc in SIDES:
        near = exists(dr, dc)

        @pl.when(near)
        def _(dr=dr, dc=dc):
            pl.semaphore_signal(
                barrier, inc=1, device_id=(me_row + dr, me_col + dc), device_id_type=pl.DeviceIdType.MESH
            )

        total = total + jnp.where(near, 1, 0)
    pl.semaphore_wait(barrier, total)

    def transfer(which, message):
        dr, dc, part = MESSAGES[message]
        rows = fields[which].shape[0] - 2 * HALO
        wide = fields[which].shape[1] - 2 * HALO
        if dr:
            from_row, to_row, n_rows = {-1: (0, HALO + rows, HALO), 1: (rows - HALO, 0, HALO)}[dr]
        else:
            from_row = (0, HALO, rows - HALO)[part]
            to_row, n_rows = HALO + from_row, (HALO, rows - 2 * HALO, HALO)[part]
        if which == 0:
            from_block = {-1: 0, 0: 0, 1: wide - 1}[dc]
            to_block = {-1: wide + 1, 0: 1, 1: 0}[dc]
            n_blocks = 1 if dc else wide
            src = x_hbm.at[pl.ds(from_row, n_rows), pl.ds(from_block, n_blocks)]
            dst = natural.at[pl.ds(to_row, n_rows), pl.ds(to_block, n_blocks)]
        elif dc == 0:
            src = fields[which].at[pl.ds(HALO + from_row, n_rows), pl.ds(HALO, wide)]
            dst = fields[which].at[pl.ds(to_row, n_rows), pl.ds(HALO, wide)]
        else:
            src = packs[which].at[pl.ds(from_row, n_rows), pl.ds((1 + dc) // 2, 1)]
            dst = edges[which].at[pl.ds(to_row, n_rows), pl.ds((1 - dc) // 2, 1)]
        return pltpu.make_async_remote_copy(
            src_ref=src,
            dst_ref=dst,
            send_sem=send_sem.at[which, message],
            recv_sem=recv_sem.at[which, message],
            device_id=(
                jnp.clip(me_row + dr, 0, count_rows - 1),
                jnp.clip(me_col + dc, 0, count_cols - 1),
            ),
            device_id_type=pl.DeviceIdType.MESH,
        )

    def send(which, messages):
        for message in messages:
            @pl.when(exists(*MESSAGES[message][:2]))
            def _(message=message):
                transfer(which, message).start()

    def arrive(which, messages):
        for message in messages:
            dr, dc, _ = MESSAGES[message]

            @pl.when(exists(-dr, -dc))
            def _(message=message):
                transfer(which, message).wait_recv()

    def sent(which):
        for message in range(len(MESSAGES)):
            @pl.when(exists(*MESSAGES[message][:2]))
            def _(message=message):
                transfer(which, message).wait_send()

    def by_side(side, act, if_top, if_bottom):
        @pl.when(side == 0)
        def _():
            act(if_top)

        @pl.when(side == 1)
        def _():
            act(if_bottom)

    early = 1 - lax.rem(me_row, 2)
    late = 1 - early

    send(0, EDGES[INNER])
    for side in (early, late):
        by_side(side, functools.partial(send, 0), EDGES[TOP] + UPWARD, EDGES[BOTTOM] + DOWNWARD)

    for field, left, right, inner in (
        (natural, 0, wide_one + 1, None),
        (h1, 0, 1, e1), (h2, 0, 1, e2), (h3, 0, 1, e3),
    ):
        rows = field.shape[0] - 2 * HALO
        row_band = jnp.zeros((HALO,) + field.shape[1:], bf16)
        col_band = jnp.zeros((field.shape[0],) + field.shape[2:], bf16)

        def clear_rows(first, field=field, inner=inner, row_band=row_band):
            field[first : first + HALO] = row_band
            if inner is not None:
                inner[first : first + HALO] = jnp.zeros((HALO,) + inner.shape[1:], bf16)

        @pl.when(me_row == 0)
        def _(clear_rows=clear_rows):
            clear_rows(0)

        @pl.when(me_row == count_rows - 1)
        def _(clear_rows=clear_rows, rows=rows):
            clear_rows(HALO + rows)

        @pl.when(me_col == 0)
        def _(field=field, col_band=col_band, left=left):
            field[:, left] = col_band

        @pl.when(me_col == count_cols - 1)
        def _(field=field, col_band=col_band, right=right):
            field[:, right] = col_band

    def pick(ref, source):
        wanted = source(lax.broadcasted_iota(jnp.int32, ref.shape, 0))
        column = lax.broadcasted_iota(jnp.int32, ref.shape, 1)
        ref[...] = jnp.where(column == wanted, 1.0, 0.0).astype(bf16)

    def slab_order(m):
        return (m & (COLS - 1)) * wide_one + (m >> 4) - HALO + COLS

    def fill_order(wide):
        def source(m):
            k, s = m >> 4, m & (COLS - 1)
            left = jnp.where(s == 0, wide * COLS + k, (wide - HALO + k) * COLS + s - 1)
            other = k - HALO
            right = jnp.where(s == COLS - 1, (wide + 1) * COLS + other, other * COLS + s + 1)
            return jnp.where(k < HALO, left, right)

        return source

    def pack_order(wide):
        def source(m):
            k = m & (COLS - 1)
            place = jnp.where(m < COLS, k * COLS, (wide - HALO + k) * COLS + COLS - 1)
            return jnp.where(k < HALO, place, -1)

        return source

    def natural_order(m):
        bits = wide_two.bit_length() - 1
        return (m & (wide_two - 1)) * COLS + (m >> bits)

    pick(order0, slab_order)
    pick(fill1, fill_order(wide_one))
    pick(fill2, fill_order(wide_two))
    pick(pack1, pack_order(wide_one))
    pick(pack2, pack_order(wide_two))
    pick(unorder, natural_order)

    def move(matrix, values):
        return jnp.dot(matrix[...], values, preferred_element_type=f32).astype(bf16)

    def spread_taps(dst, src):
        for tap in range(49):
            both = src[tap].astype(f32)
            for layer in range(both.shape[0]):
                dst[layer, tap] = jnp.broadcast_to(both[layer : layer + 1], dst.shape[2:]).astype(bf16)

    def fill(which, row):
        field = fields[which]
        wide = field.shape[1] - 2 * HALO
        c = field.shape[-1]
        if which == 0:
            values = natural[row].reshape((wide + 2) * COLS, c)
            field[row] = move(order0, values).reshape(wide + 2 * HALO, COLS, c)
            return
        inner = field[row, HALO : HALO + wide].reshape(wide * COLS, c)
        values = jnp.concatenate([inner, edges[which][row].reshape(2 * COLS, c)], axis=0)
        outer = move(fill1 if which == 1 else fill2, values).reshape(2 * HALO, COLS, c)
        field[row, 0:HALO] = outer[:HALO]
        field[row, HALO + wide : 2 * HALO + wide] = outer[HALO:]

    def store_field(which, row, n, new):
        field = fields[which]
        wide = field.shape[1] - 2 * HALO
        c = field.shape[-1]
        size = wide * COLS
        field[pl.ds(HALO + row, n), HALO : HALO + wide] = new.reshape(n, wide, COLS, c)
        for r in range(n):
            packed = move(pack1 if which == 1 else pack2, new[r * size : (r + 1) * size])
            packs[which][row + r] = packed.reshape(2, COLS, c)

    def centre(values):
        c = values.shape[-1]
        ones = jnp.full((c, c), 1.0 / c, bf16)
        mean = jnp.dot(values.astype(bf16), ones, preferred_element_type=f32)
        centred = values.astype(f32) - mean
        variance = jnp.dot((centred * centred).astype(bf16), ones, preferred_element_type=f32)
        return (centred * lax.rsqrt(variance + EPSILON)).astype(bf16)

    def gelu_twice(h):
        square = jnp.minimum(h * h, ERF_END)
        q = (ERF_FIT[2] * square + ERF_FIT[1]) * square + ERF_FIT[0]
        return h + h * jnp.tanh(h * q)

    def depthwise(field, taps, sums, layer, row, n):
        wide = field.shape[1] - 2 * HALO
        c = field.shape[-1]

        @pl.loop(0, wide)
        def _(slab):
            for lane in range(c // 128):
                lanes = slice(lane * 128, (lane + 1) * 128)
                stacks = [[] for _ in range(n)]
                for b in range(7):
                    cells = [field[row + r, slab + b, :, lanes] for r in range(n + 2 * HALO)]
                    tap = [taps[layer, 7 * a + b, :, lanes] for a in range(7)]
                    for r in range(n):
                        p = [cells[r + a] * tap[a] for a in range(7)]
                        stacks[r].append(((p[0] + p[1]) + (p[2] + p[3])) + ((p[4] + p[5]) + p[6]))
                        if b in (1, 3, 5):
                            top = stacks[r].pop()
                            stacks[r].append(stacks[r].pop() + top)
                        if b in (3, 6):
                            top = stacks[r].pop()
                            stacks[r].append(stacks[r].pop() + top)
                for r in range(n):
                    sums[r, slab, :, lanes] = stacks[r][0] + stacks[r][1]

        return sums[0:n].reshape(n * wide * COLS, c)

    def branch_rows(field, taps, w_in, w_out, sums, layer, row, n):
        flat = centre(depthwise(field, taps, sums, layer, row, n))
        hidden_size = w_in.shape[-1]
        step = 512
        total = None
        for k in range(0, hidden_size, step):
            h = jnp.dot(flat, w_in[layer, :, k : k + step], preferred_element_type=f32)
            g = gelu_twice(h.astype(bf16))
            part = jnp.dot(g, w_out[layer, k : k + step, :], preferred_element_type=f32)
            total = part if total is None else total + part
        return 0.5 * total

    def plain(field, row, n):
        wide = field.shape[1] - 2 * HALO
        c = field.shape[-1]
        return field[pl.ds(HALO + row, n), HALO : HALO + wide].astype(f32).reshape(n * wide * COLS, c)

    def section_one(layer, row, n):
        field = fields[layer]
        branch = branch_rows(field, kb1, a1, b1, sum1, layer, row, n)
        new = (plain(field, row, n) + branch).astype(bf16)
        if layer == 0:
            store_field(1, row, n, new)
            return
        normed = centre(new.astype(f32)).reshape(n, wide_one, COLS, c_one)
        for r in range(n):
            place = row + r
            first = 2 * lax.rem(place, 2)
            for q in range(wide_one):
                patches[first + q % 2, lax.div(place, 2), q // 2] = normed[r, q]

    def section_two(layer, row, n):
        field = fields[2 + layer]
        branch = branch_rows(field, kb2, a2, b2, sum2, layer, row, n)
        old = plain(field, row, n)
        mark = marks[lax.div(me_row * rows_two, TILE2), lax.div(me_col * (wide_two * COLS), TILE2)]
        keep = jnp.full(old.shape, mark, jnp.int32) == 1
        new = jnp.where(keep, old + branch, old).astype(bf16)
        if layer == 0:
            store_field(3, row, n, new)
            return
        size = wide_two * COLS
        for r in range(n):
            out_ref[row + r] = move(unorder, new[r * size : (r + 1) * size]).reshape(wide_two, COLS, c_two)

    def coarse(row, n):
        total = None
        for q in range(4):
            patch = patches[q, pl.ds(row, n)].reshape(n * wide_two * COLS, c_one)
            part = jnp.dot(patch, sk[q * c_one : (q + 1) * c_one], preferred_element_type=f32)
            total = part if total is None else total + part
        store_field(2, row, n, total.astype(bf16))

    def run(work, which, layer, rows, after_inner, after_border):
        inner = rows - 2 * HALO
        per_step = largest_divisor(inner, 5)
        steps = inner // per_step
        free_steps = max(0, steps + (-HALO // per_step))

        def border_edges(side):
            by_side(side, functools.partial(arrive, which), EDGES[TOP], EDGES[BOTTOM])
            for r in range(HALO):
                fill(which, HALO + side * (rows - HALO) + r)

        arrive(which, EDGES[INNER])

        @pl.loop(0, steps)
        def _(index):
            for r in range(per_step):
                fill(which, 2 * HALO + index * per_step + r)

        border_edges(early)

        @pl.loop(0, steps)
        def _(index):
            @pl.when(index == free_steps)
            def _():
                border_edges(late)

            place = early * (steps - 1 - index) + late * index
            work(layer, HALO + place * per_step, per_step)

        after_inner()

        @pl.loop(0, 2)
        def _(phase):
            side = lax.rem(phase + early, 2)
            by_side(side, functools.partial(arrive, which), DOWNWARD, UPWARD)
            for r in range(HALO):
                fill(which, side * (HALO + rows) + r)
            work(layer, side * (rows - HALO), HALO)
            after_border(side)

    def send_inner(which):
        send(which, EDGES[INNER])

    def send_border(which, side):
        by_side(side, functools.partial(send, which), EDGES[TOP] + UPWARD, EDGES[BOTTOM] + DOWNWARD)

    loads[1].wait()
    spread_taps(kb1, t1)
    loads[5].wait()
    spread_taps(kb2, t2)
    for index in (0, 2, 3, 4):
        loads[index].wait()
    run(
        section_one, 0, 0, rows_one,
        functools.partial(send_inner, 1), functools.partial(send_border, 1),
    )

    def coarse_inner():
        inner = rows_two - 2 * HALO
        together = largest_divisor(inner, 4)

        @pl.loop(0, inner // together)
        def _(index):
            coarse(HALO + index * together, together)

        send_inner(2)

    def coarse_border(side):
        coarse(side * (rows_two - HALO), HALO)
        send_border(2, side)

    run(section_one, 1, 1, rows_one, coarse_inner, coarse_border)
    loads[6].wait()
    loads[7].wait()
    run(
        section_two, 2, 0, rows_two,
        functools.partial(send_inner, 3), functools.partial(send_border, 3),
    )
    run(section_two, 3, 1, rows_two, lambda: None, lambda side: None)
    for which in range(4):
        sent(which)


def per_device(
    count_rows,
    count_cols,
    input_picture,
    spatial_taps_first,
    widening_matrix_first,
    narrowing_matrix_first,
    stride_kernel_matrix,
    spatial_taps_second,
    widening_matrix_second,
    narrowing_matrix_second,
    sky_clarity_marks,
):
    rows, cols, c_one = input_picture.shape
    c_two = stride_kernel_matrix.shape[1]
    half = rows // 2
    wide_one = cols // COLS
    wide_two = cols // (2 * COLS)
    weights = (
        spatial_taps_first.transpose(1, 0, 2), widening_matrix_first, narrowing_matrix_first,
        stride_kernel_matrix,
        spatial_taps_second.transpose(1, 0, 2), widening_matrix_second, narrowing_matrix_second,
    )
    vmem = pltpu.VMEM
    field_one = (rows + 2 * HALO, wide_one + 2 * HALO, COLS, c_one)
    field_two = (half + 2 * HALO, wide_two + 2 * HALO, COLS, c_two)
    layers = spatial_taps_first.shape[0]
    shapes = [
        (rows + 2 * HALO, wide_one + 2, COLS, c_one),
        field_one, field_one, field_two, field_two,
        (rows + 2 * HALO, 2, COLS, c_one),
        (half + 2 * HALO, 2, COLS, c_two),
        (half + 2 * HALO, 2, COLS, c_two),
        (rows, 2, COLS, c_one),
        (half, 2, COLS, c_two),
        (half, 2, COLS, c_two),
        *[w.shape for w in weights],
        (layers, 49, COLS, c_one),
        (layers, 49, COLS, c_two),
        (5, wide_one, COLS, c_one),
        (5, wide_two, COLS, c_two),
        ((wide_one + 2 * HALO) * COLS, (wide_one + 2) * COLS),
        (2 * HALO * COLS, (wide_one + 2) * COLS),
        (2 * HALO * COLS, (wide_two + 2) * COLS),
        (2 * COLS, wide_one * COLS),
        (2 * COLS, wide_two * COLS),
        (wide_two * COLS, wide_two * COLS),
        (4, half, wide_two, COLS, c_one),
    ]
    out = pl.pallas_call(
        functools.partial(kernel, count_rows, count_cols),
        out_shape=jax.ShapeDtypeStruct((half, wide_two, COLS, c_two), bf16),
        in_specs=[pl.BlockSpec(memory_space=pl.ANY)] * 8 + [pl.BlockSpec(memory_space=pltpu.SMEM)],
        out_specs=pl.BlockSpec(memory_space=vmem),
        scratch_shapes=[
            *[vmem(shape, bf16) for shape in shapes],
            pltpu.SemaphoreType.DMA((8,)),
            pltpu.SemaphoreType.DMA((4, len(MESSAGES))),
            pltpu.SemaphoreType.DMA((4, len(MESSAGES))),
        ],
        compiler_params=pltpu.CompilerParams(
            collective_id=0, has_side_effects=True, vmem_limit_bytes=60 * 2**20
        ),
        name="sections",
    )(input_picture.reshape(rows, wide_one, COLS, c_one), *weights, sky_clarity_marks)
    return out.reshape(half, cols // 2, c_two)


def solution(mesh):
    placed = (P("row", "col", None), P(), P(), P(), P(), P(), P(), P(), P())
    return jax.shard_map(
        functools.partial(per_device, mesh.shape["row"], mesh.shape["col"]),
        mesh=mesh, in_specs=placed, out_specs=P("row", "col", None), check_vma=False,
    )
```

```python
import functools

import jax
import jax.numpy as jnp
from jax import lax
from jax.experimental import pallas as pl
from jax.experimental.pallas import tpu as pltpu
from jax.sharding import PartitionSpec as P

TILE2 = 64
EPSILON = 1e-06
HALO = 3
COLS = 16
LANES = 128
ERF_FIT = (0.7975078823814434, 0.037005647651999776, -0.00035151703937969365)
ERF_END = 25.0
SIDES = ((-1, 0), (1, 0), (0, -1), (0, 1), (-1, -1), (-1, 1), (1, -1), (1, 1))
TOP, INNER, BOTTOM = range(3)
MESSAGES = (
    (-1, 0, None), (-1, -1, None), (-1, 1, None),
    (1, 0, None), (1, -1, None), (1, 1, None),
    (0, -1, TOP), (0, 1, TOP), (0, -1, INNER), (0, 1, INNER), (0, -1, BOTTOM), (0, 1, BOTTOM),
)
UPWARD, DOWNWARD = (0, 1, 2), (3, 4, 5)
EDGES = ((6, 7), (8, 9), (10, 11))
f32 = jnp.float32
bf16 = jnp.bfloat16


def largest_divisor(number, limit):
    return next(d for d in range(limit, 0, -1) if number % d == 0)


def lane_groups(count):
    return [slice(g * LANES, (g + 1) * LANES) for g in range(count)]


def joined(pieces):
    return jnp.concatenate([p.reshape(-1, LANES) for p in pieces], axis=1)


def kernel(
    count_rows,
    count_cols,
    x_hbm, t1_hbm, a1_hbm, b1_hbm, sk_hbm, t2_hbm, a2_hbm, b2_hbm, marks,
    out_ref,
    natural, e0, e1, e2, e3, h1, h2, h3, p1, p2, p3,
    t1, a1, b1, sk, t2, a2, b2,
    kb1, kb2, sum1, sum2,
    order0, fill1, fill2, pack1, pack2, unorder, patches,
    load_sem, send_sem, recv_sem,
):
    fields = (e0, e1, e2, e3)
    edges = (None, h1, h2, h3)
    packs = (None, p1, p2, p3)
    rows_one = e0.shape[0] - 2 * HALO
    rows_two = e2.shape[0] - 2 * HALO
    wide_one = e0.shape[1] - 2 * HALO
    wide_two = e2.shape[1] - 2 * HALO
    c_one = e0.shape[2] * LANES
    c_two = e2.shape[2] * LANES
    me_row = lax.axis_index("row")
    me_col = lax.axis_index("col")

    def exists(dr, dc):
        ok = None
        for step, me, count in ((dr, me_row, count_rows), (dc, me_col, count_cols)):
            if step == 0:
                continue
            here = me > 0 if step < 0 else me < count - 1
            ok = here if ok is None else jnp.logical_and(ok, here)
        return ok

    loads = []
    for index, (src, dst) in enumerate(
        (
            (x_hbm, natural.at[pl.ds(HALO, rows_one), pl.ds(1, wide_one)]),
            (t1_hbm, t1), (a1_hbm, a1), (b1_hbm, b1),
            (sk_hbm, sk), (t2_hbm, t2), (a2_hbm, a2), (b2_hbm, b2),
        )
    ):
        copy = pltpu.make_async_copy(src, dst, load_sem.at[index])
        copy.start()
        loads.append(copy)

    barrier = pltpu.get_barrier_semaphore()
    total = jnp.int32(0)
    for dr, dc in SIDES:
        near = exists(dr, dc)

        @pl.when(near)
        def _(dr=dr, dc=dc):
            pl.semaphore_signal(
                barrier, inc=1, device_id=(me_row + dr, me_col + dc), device_id_type=pl.DeviceIdType.MESH
            )

        total = total + jnp.where(near, 1, 0)
    pl.semaphore_wait(barrier, total)

    def transfer(which, message):
        dr, dc, part = MESSAGES[message]
        rows = fields[which].shape[0] - 2 * HALO
        wide = fields[which].shape[1] - 2 * HALO
        if dr:
            from_row, to_row, n_rows = {-1: (0, HALO + rows, HALO), 1: (rows - HALO, 0, HALO)}[dr]
        else:
            from_row = (0, HALO, rows - HALO)[part]
            to_row, n_rows = HALO + from_row, (HALO, rows - 2 * HALO, HALO)[part]
        if which == 0:
            from_block = {-1: 0, 0: 0, 1: wide - 1}[dc]
            to_block = {-1: wide + 1, 0: 1, 1: 0}[dc]
            n_blocks = 1 if dc else wide
            src = x_hbm.at[pl.ds(from_row, n_rows), pl.ds(from_block, n_blocks)]
            dst = natural.at[pl.ds(to_row, n_rows), pl.ds(to_block, n_blocks)]
        elif dc == 0:
            src = fields[which].at[pl.ds(HALO + from_row, n_rows), pl.ds(HALO, wide)]
            dst = fields[which].at[pl.ds(to_row, n_rows), pl.ds(HALO, wide)]
        else:
            src = packs[which].at[pl.ds(from_row, n_rows), pl.ds((1 + dc) // 2, 1)]
            dst = edges[which].at[pl.ds(to_row, n_rows), pl.ds((1 - dc) // 2, 1)]
        return pltpu.make_async_remote_copy(
            src_ref=src,
            dst_ref=dst,
            send_sem=send_sem.at[which, message],
            recv_sem=recv_sem.at[which, message],
            device_id=(
                jnp.clip(me_row + dr, 0, count_rows - 1),
                jnp.clip(me_col + dc, 0, count_cols - 1),
            ),
            device_id_type=pl.DeviceIdType.MESH,
        )

    def send(which, messages):
        for message in messages:
            @pl.when(exists(*MESSAGES[message][:2]))
            def _(message=message):
                transfer(which, message).start()

    def arrive(which, messages):
        for message in messages:
            dr, dc, _ = MESSAGES[message]

            @pl.when(exists(-dr, -dc))
            def _(message=message):
                transfer(which, message).wait_recv()

    def sent(which):
        for message in range(len(MESSAGES)):
            @pl.when(exists(*MESSAGES[message][:2]))
            def _(message=message):
                transfer(which, message).wait_send()

    def by_side(side, act, if_top, if_bottom):
        @pl.when(side == 0)
        def _():
            act(if_top)

        @pl.when(side == 1)
        def _():
            act(if_bottom)

    early = 1 - lax.rem(me_row, 2)
    late = 1 - early

    send(0, EDGES[INNER])
    for side in (early, late):
        by_side(side, functools.partial(send, 0), EDGES[TOP] + UPWARD, EDGES[BOTTOM] + DOWNWARD)

    for field, left, right, inner in (
        (natural, 0, wide_one + 1, None),
        (h1, 0, 1, e1), (h2, 0, 1, e2), (h3, 0, 1, e3),
    ):
        rows = field.shape[0] - 2 * HALO
        row_band = jnp.zeros((HALO,) + field.shape[1:], bf16)
        col_band = jnp.zeros((field.shape[0],) + field.shape[2:], bf16)

        def clear_rows(first, field=field, inner=inner, row_band=row_band):
            field[first : first + HALO] = row_band
            if inner is not None:
                inner[first : first + HALO] = jnp.zeros((HALO,) + inner.shape[1:], bf16)

        @pl.when(me_row == 0)
        def _(clear_rows=clear_rows):
            clear_rows(0)

        @pl.when(me_row == count_rows - 1)
        def _(clear_rows=clear_rows, rows=rows):
            clear_rows(HALO + rows)

        @pl.when(me_col == 0)
        def _(field=field, col_band=col_band, left=left):
            field[:, left] = col_band

        @pl.when(me_col == count_cols - 1)
        def _(field=field, col_band=col_band, right=right):
            field[:, right] = col_band

    def pick(ref, source):
        wanted = source(lax.broadcasted_iota(jnp.int32, ref.shape, 0))
        column = lax.broadcasted_iota(jnp.int32, ref.shape, 1)
        ref[...] = jnp.where(column == wanted, 1.0, 0.0).astype(bf16)

    def slab_order(m):
        return (m & (COLS - 1)) * wide_one + (m >> 4) - HALO + COLS

    def fill_order(wide):
        def source(m):
            k, s = m >> 4, m & (COLS - 1)
            left = jnp.where(s == 0, wide * COLS + k, (wide - HALO + k) * COLS + s - 1)
            other = k - HALO
            right = jnp.where(s == COLS - 1, (wide + 1) * COLS + other, other * COLS + s + 1)
            return jnp.where(k < HALO, left, right)

        return source

    def pack_order(wide):
        def source(m):
            k = m & (COLS - 1)
            place = jnp.where(m < COLS, k * COLS, (wide - HALO + k) * COLS + COLS - 1)
            return jnp.where(k < HALO, place, -1)

        return source

    def natural_order(m):
        bits = wide_two.bit_length() - 1
        return (m & (wide_two - 1)) * COLS + (m >> bits)

    pick(order0, slab_order)
    pick(fill1, fill_order(wide_one))
    pick(fill2, fill_order(wide_two))
    pick(pack1, pack_order(wide_one))
    pick(pack2, pack_order(wide_two))
    pick(unorder, natural_order)

    def move(matrix, values):
        return jnp.dot(matrix[...], values, preferred_element_type=f32).astype(bf16)

    def spread_taps(dst, src):
        for tap in range(49):
            both = src[tap].astype(f32)
            for layer in range(both.shape[0]):
                for g, lanes in enumerate(lane_groups(dst.shape[2])):
                    dst[layer, tap, g] = jnp.broadcast_to(both[layer : layer + 1, lanes], (COLS, LANES)).astype(bf16)

    def fill(which, row):
        field = fields[which]
        wide = field.shape[1] - 2 * HALO
        groups = lane_groups(field.shape[2])
        c = len(groups) * LANES
        if which == 0:
            whole = move(order0, natural[row].reshape((wide + 2) * COLS, c))
            for g, lanes in enumerate(groups):
                field[row, :, g] = whole[:, lanes].reshape(wide + 2 * HALO, COLS, LANES)
            return
        inner = joined([field[row, HALO : HALO + wide, g] for g in range(len(groups))])
        values = jnp.concatenate([inner, edges[which][row].reshape(2 * COLS, c)], axis=0)
        outer = move(fill1 if which == 1 else fill2, values)
        for g, lanes in enumerate(groups):
            part = outer[:, lanes].reshape(2 * HALO, COLS, LANES)
            field[row, 0:HALO, g] = part[:HALO]
            field[row, HALO + wide : 2 * HALO + wide, g] = part[HALO:]

    def store_field(which, row, n, new):
        field = fields[which]
        wide = field.shape[1] - 2 * HALO
        c = field.shape[2] * LANES
        size = wide * COLS
        for g, lanes in enumerate(lane_groups(field.shape[2])):
            field[pl.ds(HALO + row, n), HALO : HALO + wide, g] = new[:, lanes].reshape(n, wide, COLS, LANES)
        for r in range(n):
            packed = move(pack1 if which == 1 else pack2, new[r * size : (r + 1) * size])
            packs[which][row + r] = packed.reshape(2, COLS, c)

    def centre(values):
        c = values.shape[-1]
        ones = jnp.full((c, c), 1.0 / c, bf16)
        mean = jnp.dot(values.astype(bf16), ones, preferred_element_type=f32)
        centred = values.astype(f32) - mean
        variance = jnp.dot((centred * centred).astype(bf16), ones, preferred_element_type=f32)
        return (centred * lax.rsqrt(variance + EPSILON)).astype(bf16)

    def gelu_twice(h):
        square = jnp.minimum(h * h, ERF_END)
        q = (ERF_FIT[2] * square + ERF_FIT[1]) * square + ERF_FIT[0]
        return h + h * jnp.tanh(h * q)

    def depthwise(field, taps, sums, layer, row, n):
        wide = field.shape[1] - 2 * HALO
        groups = field.shape[2]

        @pl.loop(0, wide)
        def _(slab):
            for g in range(groups):
                stacks = [[] for _ in range(n)]
                for b in range(7):
                    cells = [field[row + r, slab + b, g] for r in range(n + 2 * HALO)]
                    tap = [taps[layer, 7 * a + b, g] for a in range(7)]
                    for r in range(n):
                        p = [cells[r + a] * tap[a] for a in range(7)]
                        stacks[r].append(((p[0] + p[1]) + (p[2] + p[3])) + ((p[4] + p[5]) + p[6]))
                        if b in (1, 3, 5):
                            top = stacks[r].pop()
                            stacks[r].append(stacks[r].pop() + top)
                        if b in (3, 6):
                            top = stacks[r].pop()
                            stacks[r].append(stacks[r].pop() + top)
                for r in range(n):
                    sums[r, slab, g] = stacks[r][0] + stacks[r][1]

        return joined([sums[0:n, :, g] for g in range(groups)])

    def branch_rows(field, taps, w_in, w_out, sums, layer, row, n):
        flat = centre(depthwise(field, taps, sums, layer, row, n))
        hidden_size = w_in.shape[-1]
        step = 512
        total = None
        for k in range(0, hidden_size, step):
            h = jnp.dot(flat, w_in[layer, :, k : k + step], preferred_element_type=f32)
            g = gelu_twice(h.astype(bf16))
            part = jnp.dot(g, w_out[layer, k : k + step, :], preferred_element_type=f32)
            total = part if total is None else total + part
        return 0.5 * total

    def plain(field, row, n):
        wide = field.shape[1] - 2 * HALO
        pieces = [field[pl.ds(HALO + row, n), HALO : HALO + wide, g] for g in range(field.shape[2])]
        return joined(pieces).astype(f32)

    def section_one(layer, row, n):
        field = fields[layer]
        branch = branch_rows(field, kb1, a1, b1, sum1, layer, row, n)
        new = (plain(field, row, n) + branch).astype(bf16)
        if layer == 0:
            store_field(1, row, n, new)
            return
        normed = centre(new.astype(f32)).reshape(n, wide_one, COLS, c_one)
        for r in range(n):
            place = row + r
            first = 2 * lax.rem(place, 2)
            for q in range(wide_one):
                patches[first + q % 2, lax.div(place, 2), q // 2] = normed[r, q]

    def section_two(layer, row, n):
        field = fields[2 + layer]
        branch = branch_rows(field, kb2, a2, b2, sum2, layer, row, n)
        old = plain(field, row, n)
        mark = marks[lax.div(me_row * rows_two, TILE2), lax.div(me_col * (wide_two * COLS), TILE2)]
        keep = jnp.full(old.shape, mark, jnp.int32) == 1
        new = jnp.where(keep, old + branch, old).astype(bf16)
        if layer == 0:
            store_field(3, row, n, new)
            return
        size = wide_two * COLS
        for r in range(n):
            out_ref[row + r] = move(unorder, new[r * size : (r + 1) * size]).reshape(wide_two, COLS, c_two)

    def coarse(row, n):
        total = None
        for q in range(4):
            patch = patches[q, pl.ds(row, n)].reshape(n * wide_two * COLS, c_one)
            part = jnp.dot(patch, sk[q * c_one : (q + 1) * c_one], preferred_element_type=f32)
            total = part if total is None else total + part
        store_field(2, row, n, total.astype(bf16))

    def run(work, which, layer, rows, after_inner, after_border):
        inner = rows - 2 * HALO
        per_step = largest_divisor(inner, 5)
        steps = inner // per_step
        free_steps = max(0, steps + (-HALO // per_step))

        def border_edges(side):
            by_side(side, functools.partial(arrive, which), EDGES[TOP], EDGES[BOTTOM])
            for r in range(HALO):
                fill(which, HALO + side * (rows - HALO) + r)

        arrive(which, EDGES[INNER])

        @pl.loop(0, steps)
        def _(index):
            for r in range(per_step):
                fill(which, 2 * HALO + index * per_step + r)

        border_edges(early)

        @pl.loop(0, steps)
        def _(index):
            @pl.when(index == free_steps)
            def _():
                border_edges(late)

            place = early * (steps - 1 - index) + late * index
            work(layer, HALO + place * per_step, per_step)

        after_inner()

        @pl.loop(0, 2)
        def _(phase):
            side = lax.rem(phase + early, 2)
            by_side(side, functools.partial(arrive, which), DOWNWARD, UPWARD)
            for r in range(HALO):
                fill(which, side * (HALO + rows) + r)
            work(layer, side * (rows - HALO), HALO)
            after_border(side)

    def send_inner(which):
        send(which, EDGES[INNER])

    def send_border(which, side):
        by_side(side, functools.partial(send, which), EDGES[TOP] + UPWARD, EDGES[BOTTOM] + DOWNWARD)

    loads[1].wait()
    spread_taps(kb1, t1)
    loads[5].wait()
    spread_taps(kb2, t2)
    for index in (0, 2, 3, 4):
        loads[index].wait()
    run(
        section_one, 0, 0, rows_one,
        functools.partial(send_inner, 1), functools.partial(send_border, 1),
    )

    def coarse_inner():
        inner = rows_two - 2 * HALO
        together = largest_divisor(inner, 4)

        @pl.loop(0, inner // together)
        def _(index):
            coarse(HALO + index * together, together)

        send_inner(2)

    def coarse_border(side):
        coarse(side * (rows_two - HALO), HALO)
        send_border(2, side)

    run(section_one, 1, 1, rows_one, coarse_inner, coarse_border)
    loads[6].wait()
    loads[7].wait()
    run(
        section_two, 2, 0, rows_two,
        functools.partial(send_inner, 3), functools.partial(send_border, 3),
    )
    run(section_two, 3, 1, rows_two, lambda: None, lambda side: None)
    for which in range(4):
        sent(which)


def per_device(
    count_rows,
    count_cols,
    input_picture,
    spatial_taps_first,
    widening_matrix_first,
    narrowing_matrix_first,
    stride_kernel_matrix,
    spatial_taps_second,
    widening_matrix_second,
    narrowing_matrix_second,
    sky_clarity_marks,
):
    rows, cols, c_one = input_picture.shape
    c_two = stride_kernel_matrix.shape[1]
    half = rows // 2
    wide_one = cols // COLS
    wide_two = cols // (2 * COLS)
    weights = (
        spatial_taps_first.transpose(1, 0, 2), widening_matrix_first, narrowing_matrix_first,
        stride_kernel_matrix,
        spatial_taps_second.transpose(1, 0, 2), widening_matrix_second, narrowing_matrix_second,
    )
    vmem = pltpu.VMEM
    field_one = (rows + 2 * HALO, wide_one + 2 * HALO, c_one // LANES, COLS, LANES)
    field_two = (half + 2 * HALO, wide_two + 2 * HALO, c_two // LANES, COLS, LANES)
    layers = spatial_taps_first.shape[0]
    shapes = [
        (rows + 2 * HALO, wide_one + 2, COLS, c_one),
        field_one, field_one, field_two, field_two,
        (rows + 2 * HALO, 2, COLS, c_one),
        (half + 2 * HALO, 2, COLS, c_two),
        (half + 2 * HALO, 2, COLS, c_two),
        (rows, 2, COLS, c_one),
        (half, 2, COLS, c_two),
        (half, 2, COLS, c_two),
        *[w.shape for w in weights],
        (layers, 49, c_one // LANES, COLS, LANES),
        (layers, 49, c_two // LANES, COLS, LANES),
        (5, wide_one, c_one // LANES, COLS, LANES),
        (5, wide_two, c_two // LANES, COLS, LANES),
        ((wide_one + 2 * HALO) * COLS, (wide_one + 2) * COLS),
        (2 * HALO * COLS, (wide_one + 2) * COLS),
        (2 * HALO * COLS, (wide_two + 2) * COLS),
        (2 * COLS, wide_one * COLS),
        (2 * COLS, wide_two * COLS),
        (wide_two * COLS, wide_two * COLS),
        (4, half, wide_two, COLS, c_one),
    ]
    out = pl.pallas_call(
        functools.partial(kernel, count_rows, count_cols),
        out_shape=jax.ShapeDtypeStruct((half, wide_two, COLS, c_two), bf16),
        in_specs=[pl.BlockSpec(memory_space=pl.ANY)] * 8 + [pl.BlockSpec(memory_space=pltpu.SMEM)],
        out_specs=pl.BlockSpec(memory_space=vmem),
        scratch_shapes=[
            *[vmem(shape, bf16) for shape in shapes],
            pltpu.SemaphoreType.DMA((8,)),
            pltpu.SemaphoreType.DMA((4, len(MESSAGES))),
            pltpu.SemaphoreType.DMA((4, len(MESSAGES))),
        ],
        compiler_params=pltpu.CompilerParams(
            collective_id=0, has_side_effects=True, vmem_limit_bytes=60 * 2**20
        ),
        name="sections",
    )(input_picture.reshape(rows, wide_one, COLS, c_one), *weights, sky_clarity_marks)
    return out.reshape(half, cols // 2, c_two)


def solution(mesh):
    placed = (P("row", "col", None), P(), P(), P(), P(), P(), P(), P(), P())
    return jax.shard_map(
        functools.partial(per_device, mesh.shape["row"], mesh.shape["col"]),
        mesh=mesh, in_specs=placed, out_specs=P("row", "col", None), check_vma=False,
    )
```
